256 devices in a mesh: prow: 8 (over y, core), pcol: 32 (over z, x).
Axes of the slice: x: 4, y: 4, z: 8, core: 2. Of those that a mesh axis runs over, the one named last changes fastest.
Arguments:
- matrix: float32 [16384, 16384], P('prow', 'pcol'), may hold values from -6 to 6
- pivots: int32 [2, 256], replicated, may hold values from 0 to 16383, as said below
- lower_inverse: float32 [2, 256, 256], replicated, as said below
- upper_inverse: float32 [2, 256, 256], replicated, as said below
Outputs:
- factored: float32 [16384, 16384], P('prow', 'pcol')
The draws below stay inside these ranges and needn't reach their ends.
Inputs may be any that keep to these rules, and one draw needn't show every extreme that they name: For panel k and position r, pivots[k, r] is either k * 256 + r or a row at or after (k + 1) * 256; the rows of the second kind are distinct within a panel. `lower_inverse`: unit lower triangular. `upper_inverse`: upper triangular with a positive diagonal.
All inputs are finite; a program needn't handle non-finite values.
Results may differ from the reference program's by a relative error of at most 0.00012.
Values sent between devices are 32-bit elements; how exact they have to be, the bound alone decides.
No kernel may reach another device: no remote copies, remote signals or barrier semaphores. Data moves between devices by JAX's collectives and lax.ppermute only.
A program may use at most 64 MiB of HBM per device.

```python
import math
import jax
import jax.numpy as jnp
from jax import lax

NB = 256
PANELS = 2
RB_DEV = 8
CB_DEV = 2
ROWS = 16384
COLS = 16384
N_PROW = 8
N_PCOL = 32


def draw_pivots(key, part):
    key = jax.random.fold_in(key, 11)
    rows_list = []
    for panel_index in range(PANELS):
        draw_key = jax.random.fold_in(key, panel_index)
        key_perm, key_order, key_keep = jax.random.split(draw_key, 3)
        base_row = (panel_index + 1) * NB
        row_span = ROWS - base_row - 1
        picked = jax.random.permutation(key_perm, row_span)[:NB - 1].astype(jnp.int32) + base_row
        candidates = jnp.concatenate([picked, jnp.full((1,), ROWS - 1, jnp.int32)])
        candidates = candidates[jax.random.permutation(key_order, NB)]
        own_rows = panel_index * NB + jnp.arange(NB, dtype=jnp.int32)
        keep_own = jax.random.randint(key_keep, (NB,), 0, 5) == 0
        keep_own = jnp.logical_and(keep_own, candidates != ROWS - 1)
        rows_list.append(jnp.where(keep_own, own_rows, candidates))
    return jnp.stack(rows_list).astype(jnp.int32)


def draw_lower_inverse(key, part):
    key = jax.random.fold_in(key, 23)
    shape = (PANELS, NB, NB)
    noise = jax.random.normal(key, shape, jnp.float32)
    row_ids = lax.broadcasted_iota(jnp.int32, shape, 1)
    col_ids = lax.broadcasted_iota(jnp.int32, shape, 2)
    strict = row_ids > col_ids
    ones = jnp.where(row_ids == col_ids, 1.0, 0.0).astype(jnp.float32)
    return ones + jnp.where(strict, noise / math.sqrt(NB), 0.0).astype(jnp.float32)


def draw_upper_inverse(key, part):
    key = jax.random.fold_in(key, 37)
    key_diag, key_noise = jax.random.split(key)
    shape = (PANELS, NB, NB)
    diagonal = jax.random.uniform(key_diag, shape, jnp.float32, 1.0, 2.0)
    noise = jax.random.normal(key_noise, shape, jnp.float32)
    row_ids = lax.broadcasted_iota(jnp.int32, shape, 1)
    col_ids = lax.broadcasted_iota(jnp.int32, shape, 2)
    values = jnp.where(row_ids == col_ids, diagonal, 0.0)
    values = values + jnp.where(row_ids < col_ids, noise * 2.4 / math.sqrt(NB), 0.0)
    return (values * (0.5 / math.sqrt(NB))).astype(jnp.float32)


def level_of(key, extent, pieces, least, top_value):
    def one(position, shards_of):
        draws = jax.random.uniform(jax.random.fold_in(jax.random.fold_in(key, 6), position), (shards_of,), jnp.float32, least / len(pieces), top_value / len(pieces))
        return jnp.repeat(jnp.exp(draws), extent[position] // shards_of).reshape((-1,) + (1,) * (len(extent) - position - 1))

    level = one(*pieces[0])
    for cut in pieces[1:]:
        level = level * one(*cut)
    return level


def centred(stream_key, extent, spread, reach, shards=(), held_as=jnp.bfloat16):
    result = spread * jax.random.normal(stream_key, extent, jnp.float32)
    if shards:
        result = result * level_of(stream_key, extent, shards, -0.22, 0.18)
    return jnp.clip(result, -reach, reach).astype(held_as)


def setup_inputs(seed: int = 0) -> dict:
    seeds = jax.random.split(jax.random.key(seed), 5)
    matrix = centred(seeds[0], (ROWS, COLS), 1.0, 6.0, ((0, 8), (1, 32)), jnp.float32)
    pivots = draw_pivots(jax.random.fold_in(seeds[4], 71), 0)
    lower_inverse = draw_lower_inverse(jax.random.fold_in(seeds[4], 71), 0)
    upper_inverse = draw_upper_inverse(jax.random.fold_in(seeds[4], 71), 0)
    return dict(matrix=matrix, pivots=pivots, lower_inverse=lower_inverse, upper_inverse=upper_inverse)


def exact_dot(left, right):
    return jnp.dot(left, right, precision=lax.Precision.HIGHEST, preferred_element_type=jnp.float32)


def to_logical(stored):
    by_rows = stored.reshape(N_PROW, RB_DEV, NB, COLS).transpose(1, 0, 2, 3).reshape(ROWS, COLS)
    return by_rows.reshape(ROWS, N_PCOL, CB_DEV, NB).transpose(0, 2, 1, 3).reshape(ROWS, COLS)


def from_logical(logical):
    by_rows = logical.reshape(RB_DEV, N_PROW, NB, COLS).transpose(1, 0, 2, 3).reshape(ROWS, COLS)
    return by_rows.reshape(ROWS, CB_DEV, N_PCOL, NB).transpose(0, 2, 1, 3).reshape(ROWS, COLS)


def reference(matrix, pivots, lower_inverse, upper_inverse):
    current = to_logical(matrix)
    for panel_index in range(PANELS):
        start_col = panel_index * NB
        stop_col = start_col + NB
        chosen_rows = pivots[panel_index]
        initial_top = current[start_col:stop_col]
        chosen_values = current[chosen_rows]
        current = current.at[chosen_rows].set(initial_top)
        current = current.at[start_col:stop_col].set(chosen_values)
        lower_part = exact_dot(current[stop_col:, start_col:stop_col], upper_inverse[panel_index])
        upper_part = exact_dot(lower_inverse[panel_index], current[start_col:stop_col, stop_col:])
        trailing = current[stop_col:, stop_col:] - exact_dot(lower_part, upper_part)
        current = current.at[stop_col:, stop_col:].set(trailing)
        current = current.at[stop_col:, start_col:stop_col].set(lower_part)
        current = current.at[start_col:stop_col, stop_col:].set(upper_part)
    return from_logical(current)
```

```python
import jax
import jax.numpy as jnp
from jax import lax
from jax.sharding import PartitionSpec as P

NZ, NX, NY, NCORE = 8, 4, 4, 2


def dot(left, right, precision=lax.Precision.HIGHEST):
    return jnp.dot(left, right, precision=precision, preferred_element_type=jnp.float32)


def at(z, x):
    return z % NZ * NX + x % NX


def along_y(step):
    return [
        (y * NCORE + c, (y + step) % NY * NCORE + c) for y in range(NY) for c in range(NCORE)
    ]


def other_core():
    return [(y * NCORE + c, y * NCORE + 1 - c) for y in range(NY) for c in range(NCORE)]


def pick(index, options):
    value = options[0]
    for place in range(1, len(options)):
        value = jnp.where(index == place, options[place], value)
    return value


def down_z(z, pieces):
    arrived = [pieces[0]]
    for k in range(1, NZ):
        arrived.append(lax.ppermute(pieces[k], "pcol", [(at(0, 0), at(k, 0)), (at(0, 1), at(k, 1))]))
    return pick(z, arrived)


def across_x(x, mine):
    zs = range(NZ)
    plus = lax.ppermute(
        mine, "pcol", [(at(z, 0), at(z, 1)) for z in zs] + [(at(z, 1), at(z, 2)) for z in zs]
    )
    minus = lax.ppermute(
        mine, "pcol", [(at(z, 0), at(z, 3)) for z in zs] + [(at(z, 1), at(z, 0)) for z in zs]
    )
    twice = lax.ppermute(
        mine, "pcol", [(at(z, 0), at(z, 2)) for z in zs] + [(at(z, 1), at(z, 3)) for z in zs]
    )
    first = pick(x, [mine, plus, twice, minus])
    second = pick(x, [minus, mine, plus, twice])
    return jnp.concatenate([first, second], axis=1)


def gather_prow(y, core, mine):
    held = jnp.zeros((NY,) + mine.shape, mine.dtype)
    held = lax.dynamic_update_index_in_dim(held, mine, y, 0)
    for step in range(1, NY):
        got = lax.ppermute(mine, "prow", along_y(step))
        held = lax.dynamic_update_index_in_dim(held, got, (y - step) % NY, 0)
    others = lax.ppermute(held, "prow", other_core())
    return jnp.stack([jnp.where(core == 0, held, others), jnp.where(core == 0, others, held)])


def on_device(matrix, pivots, lower_inverse, upper_inverse):
    nb = lower_inverse.shape[1]
    rows = matrix.shape[0]
    n_prow = lax.axis_size("prow")
    p, q = lax.axis_index("prow"), lax.axis_index("pcol")
    y, core = p // NCORE, p % NCORE
    z, x = q // NX, q % NX
    share = 2 * nb // n_prow

    with jax.named_scope("panel_scatter"):
        piece = down_z(z, [matrix[nb * k : nb * (k + 1), :nb] for k in range(NZ)])
    with jax.named_scope("panel_across"):
        piece = across_x(x, piece)

    pivot0, pivot1 = pivots[0], pivots[1]
    order = jnp.arange(nb, dtype=jnp.int32)

    def before0(wanted):
        hit = wanted[:, None] == pivot0[None, :]
        found = jnp.sum(jnp.where(hit, order[None, :] + 1, 0), axis=1)
        return jnp.where(found > 0, found - 1, wanted)

    sources = jnp.concatenate([pivot0, before0(pivot1)])
    second_top = before0(nb + order)
    place = jnp.arange(rows, dtype=jnp.int32)
    row_ids = (place // nb * n_prow + p) * nb + place % nb
    hit1 = row_ids[:, None] == pivot1[None, :]
    hit0 = row_ids[:, None] == pivot0[None, :]
    from1 = jnp.sum(jnp.where(hit1, second_top[None, :] + 1, 0), axis=1)
    from0 = jnp.sum(jnp.where(hit0, order[None, :] + 1, 0), axis=1)
    below = row_ids >= 2 * nb
    origin = jnp.where(below, jnp.where(from1 > 0, from1, from0), 0) - 1
    kept_row = jnp.logical_and(below, origin < 0)

    with jax.named_scope("top_exchange"):
        mine = sources // nb % n_prow == p
        local = sources // nb // n_prow * nb + sources % nb
        chosen = jnp.where(mine[:, None], matrix[local], 0.0)
        sent = lax.dynamic_slice_in_dim(chosen, (1 - core) * nb, nb, 0)
        kept = lax.dynamic_slice_in_dim(chosen, core * nb, nb, 0)
        half = kept + lax.ppermute(sent, "prow", other_core())
        total = lax.dynamic_slice_in_dim(half, y * share, share, 0)
        olds = [matrix[:share]]
        for step in range(1, NY):
            to = (y + step) % NY * share
            packed = jnp.concatenate(
                [
                    lax.dynamic_slice_in_dim(half, to, share, 0),
                    lax.dynamic_slice_in_dim(matrix, to, share, 0),
                ]
            )
            got = lax.ppermute(packed, "prow", along_y(step))
            total = total + got[:share]
            olds.append(got[share:])
        slab = jnp.concatenate([total, pick(y, olds)])
    with jax.named_scope("top_gather"):
        tops = gather_prow(y, core, slab)
    with jax.named_scope("fix_down"):
        fix = down_z(z, [slab[:, :nb]] * NZ)
    with jax.named_scope("fix_across"):
        fix = across_x(x, fix)
    with jax.named_scope("fix_gather"):
        fix = gather_prow(y, core, fix)
    width = matrix.shape[1]
    top = tops[:, :, :share].reshape(2 * nb, width)
    old = tops[:, :, share:].reshape(2 * nb, width)
    top_panel = fix[:, :, :share].reshape(2 * nb, 2 * nb)
    old_panel = fix[:, :, share:].reshape(2 * nb, 2 * nb)

    with jax.named_scope("upper"):
        column = jnp.arange(width, dtype=jnp.int32)[None, :]
        in_first = jnp.logical_and(q == 0, column < nb)
        in_second = jnp.logical_and(q == 1, column < nb)
        keep = jnp.logical_not(jnp.logical_or(in_first, in_second))
        minus_one = jnp.where(
            lax.broadcasted_iota(jnp.int32, (nb, width), 0)
            == lax.broadcasted_iota(jnp.int32, (nb, width), 1),
            -1.0,
            0.0,
        ).astype(jnp.float32)
        upper0 = dot(lower_inverse[0], top[:nb])
        lower_top = dot(top_panel[nb:, :nb], upper_inverse[0])
        cross = dot(lower_inverse[0], top_panel[:nb, nb:])
        swapped1 = top[nb:] - dot(lower_top, upper0)
        upper1 = dot(lower_inverse[1], swapped1)
        use0 = jnp.where(in_first, minus_one, jnp.where(in_second, 0.0, upper0))
        use1 = jnp.where(in_second, minus_one, jnp.where(in_first, 0.0, upper1))
        solved1 = dot(upper_inverse[1], use1)
        solved0 = dot(upper_inverse[0], use0 - dot(cross, solved1))
        factor = jnp.concatenate([solved0, solved1])
        lower_wide = jnp.concatenate([lower_top] * (width // nb), axis=1)
        top0 = jnp.where(in_first, top[:nb], upper0)
        top1 = jnp.where(in_first, lower_wide, jnp.where(in_second, swapped1, upper1))

    with jax.named_scope("base"):
        moved = jnp.where(keep, old, 0.0) - dot(old_panel, factor)
        select = (origin[:, None] == jnp.arange(2 * nb, dtype=jnp.int32)[None, :]).astype(jnp.float32)
        base = jnp.where(jnp.logical_and(keep, kept_row[:, None]), matrix, 0.0) + dot(select, moved)
        head = jnp.where(p == 0, top0, jnp.where(p == 1, top1, base[:nb]))
        base = base.at[:nb].set(head)

    with jax.named_scope("panel_gather"):
        panel = lax.all_gather(
            piece,
            "pcol",
            axis_index_groups=[[at(k, j) for k in range(NZ)] for j in range(NX)],
            tiled=True,
        )
    with jax.named_scope("update"):
        product = dot(panel, factor, lax.Precision.HIGH)
        return base - jnp.where(kept_row[:, None], product, 0.0)


def solution(mesh):
    in_specs = (P("prow", "pcol"), P(), P(), P())
    out_specs = P("prow", "pcol")
    return jax.shard_map(
        on_device, mesh=mesh, in_specs=in_specs, out_specs=out_specs, check_vma=False
    )
```

```python
import functools

import jax
import jax.numpy as jnp
from jax import lax
from jax.experimental import pallas as pl
from jax.experimental.pallas import tpu as pltpu
from jax.sharding import PartitionSpec as P

NZ, NX, NY, NCORE = 8, 4, 4, 2


def dot(left, right, precision=lax.Precision.HIGHEST):
    return jnp.dot(left, right, precision=precision, preferred_element_type=jnp.float32)


def at(z, x):
    return z % NZ * NX + x % NX


def along_z(step):
    return [(at(z, x), at(z + step, x)) for z in range(NZ) for x in range(NX)]


def along_y(step):
    return [
        (y * NCORE + c, (y + step) % NY * NCORE + c) for y in range(NY) for c in range(NCORE)
    ]


def other_core():
    return [(y * NCORE + c, y * NCORE + 1 - c) for y in range(NY) for c in range(NCORE)]


def pick(index, options):
    value = options[0]
    for place in range(1, len(options)):
        value = jnp.where(index == place, options[place], value)
    return value


def down_z(z, pieces):
    arrived = [pieces[0]]
    for k in range(1, NZ):
        arrived.append(lax.ppermute(pieces[k], "pcol", [(at(0, 0), at(k, 0)), (at(0, 1), at(k, 1))]))
    return pick(z, arrived)


def across_x(x, mine):
    zs = range(NZ)
    plus = lax.ppermute(
        mine, "pcol", [(at(z, 0), at(z, 1)) for z in zs] + [(at(z, 1), at(z, 2)) for z in zs]
    )
    minus = lax.ppermute(
        mine, "pcol", [(at(z, 0), at(z, 3)) for z in zs] + [(at(z, 1), at(z, 0)) for z in zs]
    )
    twice = lax.ppermute(
        mine, "pcol", [(at(z, 0), at(z, 2)) for z in zs] + [(at(z, 1), at(z, 3)) for z in zs]
    )
    first = pick(x, [mine, plus, twice, minus])
    second = pick(x, [minus, mine, plus, twice])
    return jnp.concatenate([first, second], axis=1)


def gather_y(mine):
    return jnp.stack([mine] + [lax.ppermute(mine, "prow", along_y(k)) for k in range(1, NY)])


def split(value):
    high = value.astype(jnp.bfloat16)
    return high, (value - high.astype(jnp.float32)).astype(jnp.bfloat16)


def factor_kernel(
    ids, top_mine, top_other, fix_mine, fix_other, lower_inverse, upper_inverse,
    factor_high, factor_low, moved_high, moved_low, head,
):
    p, q, y, core = ids[0], ids[1], ids[2], ids[3]
    nb = lower_inverse.shape[1]
    share = top_mine.shape[1] // 2
    width = top_mine.shape[2]

    def rows(mine, other, which, part):
        held = []
        for owner in range(NY):
            back = lax.rem(y - owner + NY, NY)
            held.append(
                jnp.where(
                    core == which,
                    mine[back, part * share : (part + 1) * share, :],
                    other[back, part * share : (part + 1) * share, :],
                )
            )
        return jnp.concatenate(held, axis=0)

    first, second = rows(top_mine, top_other, 0, 0), rows(top_mine, top_other, 1, 0)
    cross_rows = rows(fix_mine, fix_other, 0, 0)[:, nb:]
    panel_rows = rows(fix_mine, fix_other, 1, 0)[:, :nb]
    row = lax.broadcasted_iota(jnp.int32, (nb, width), 0)
    column = lax.broadcasted_iota(jnp.int32, (nb, width), 1)
    in_first = jnp.logical_and(q == 0, column < nb)
    in_second = jnp.logical_and(q == 1, column < nb)
    minus_one = jnp.where(row == column, -1.0, 0.0).astype(jnp.float32)
    upper0 = dot(lower_inverse[0], first)
    lower_top = dot(panel_rows, upper_inverse[0])
    cross = dot(lower_inverse[0], cross_rows)
    swapped1 = second - dot(lower_top, upper0)
    upper1 = dot(lower_inverse[1], swapped1)
    use0 = jnp.where(in_first, minus_one, jnp.where(in_second, 0.0, upper0))
    use1 = jnp.where(in_second, minus_one, jnp.where(in_first, 0.0, upper1))
    solved1 = dot(upper_inverse[1], use1)
    solved0 = dot(upper_inverse[0], use0 - dot(cross, solved1))
    high0, low0 = split(solved0)
    high1, low1 = split(solved1)
    factor_high[:nb], factor_high[nb:] = high0, high1
    factor_low[:nb], factor_low[nb:] = low0, low1
    lower_wide = jnp.concatenate([lower_top] * (width // nb), axis=1)
    top0 = jnp.where(in_first, first, upper0)
    top1 = jnp.where(in_first, lower_wide, jnp.where(in_second, swapped1, upper1))
    head[...] = jnp.where(p == 0, top0, top1)
    drop = jnp.logical_or(in_first, in_second)
    for which in range(NCORE):
        old = jnp.where(drop, 0.0, rows(top_mine, top_other, which, 1))
        panel_part = rows(fix_mine, fix_other, which, 1)
        moved = old - dot(panel_part[:, :nb], solved0) - dot(panel_part[:, nb:], solved1)
        high, low = split(moved)
        moved_high[which * nb : (which + 1) * nb] = high
        moved_low[which * nb : (which + 1) * nb] = low


def update_kernel(
    ids, origin, factor_high, factor_low, moved_high, moved_low, head, *rest
):
    pieces = rest[: NZ + 1]
    matrix, out, matrix_block, out_block, matrix_sem, out_sem = rest[NZ + 1 :]
    p, q = ids[0], ids[1]
    z = lax.div(q, NX)
    nb, width = head.shape
    one = functools.partial(jnp.dot, preferred_element_type=jnp.float32)
    column = lax.broadcasted_iota(jnp.int32, (nb, width), 1)
    drop = jnp.logical_and(q < 2, column < nb)
    owners = [lax.rem(z + step + NZ, NZ) for step in (0, -1, 1, -2, 2, -3, 3, NZ // 2)]

    def place(i):
        return pl.ds(pl.multiple_of(owners[i] * nb, nb), nb)

    def matrix_copy(i):
        return pltpu.make_async_copy(matrix.at[place(i)], matrix_block.at[i % 2], matrix_sem.at[i % 2])

    def out_copy(i):
        return pltpu.make_async_copy(out_block.at[i % 2], out.at[place(i)], out_sem.at[i % 2])

    for i in range(2):
        matrix_copy(i).start()
    for i in range(NZ):
        matrix_copy(i).wait()
        if i >= 2:
            out_copy(i - 2).wait()
        if i < NZ - 1:
            panel = pieces[i][...]
        else:
            panel = jnp.concatenate([pieces[i][...], pieces[i + 1][...]], axis=0)
        high, low = split(panel)
        product = (
            one(high, factor_high[...]) + one(high, factor_low[...]) + one(low, factor_high[...])
        )
        source = origin[place(i), :]
        places = lax.broadcasted_iota(jnp.int32, (nb, 2 * nb), 1)
        chosen = jnp.where(source == places, 1.0, 0.0).astype(jnp.bfloat16)
        moved = one(chosen, moved_high[...]) + one(chosen, moved_low[...])
        kept = jnp.where(drop, 0.0, matrix_block[i % 2]) - product
        value = jnp.where(source >= 0, moved, kept)
        is_head = jnp.logical_and(owners[i] == 0, p < 2)
        out_block[i % 2] = jnp.where(is_head, head[...], value)
        out_copy(i).start()
        if i + 2 < NZ:
            matrix_copy(i + 2).start()
    for i in (NZ - 2, NZ - 1):
        out_copy(i).wait()


def on_device(matrix, pivots, lower_inverse, upper_inverse):
    nb = lower_inverse.shape[1]
    rows = matrix.shape[0]
    n_prow = lax.axis_size("prow")
    p, q = lax.axis_index("prow"), lax.axis_index("pcol")
    y, core = p // NCORE, p % NCORE
    z, x = q // NX, q % NX
    share = 2 * nb // n_prow

    with jax.named_scope("panel_scatter"):
        piece = down_z(z, [matrix[nb * k : nb * (k + 1), :nb] for k in range(NZ)])

    pivot0, pivot1 = pivots[0], pivots[1]
    order = jnp.arange(nb, dtype=jnp.int32)

    def before0(wanted):
        hit = wanted[:, None] == pivot0[None, :]
        found = jnp.sum(jnp.where(hit, order[None, :] + 1, 0), axis=1)
        return jnp.where(found > 0, found - 1, wanted)

    sources = jnp.concatenate([pivot0, before0(pivot1)])
    second_top = before0(nb + order)
    place = lax.broadcasted_iota(jnp.int32, (rows, 1), 0)
    row_ids = (place // nb * n_prow + p) * nb + place % nb
    hit1 = row_ids == pivot1[None, :]
    hit0 = row_ids == pivot0[None, :]
    from1 = jnp.sum(jnp.where(hit1, second_top[None, :] + 1, 0), axis=1, keepdims=True)
    from0 = jnp.sum(jnp.where(hit0, order[None, :] + 1, 0), axis=1, keepdims=True)
    origin = jnp.where(row_ids >= 2 * nb, jnp.where(from1 > 0, from1, from0), 0) - 1

    with jax.named_scope("top_exchange"):
        mine = sources // nb % n_prow == p
        local = sources // nb // n_prow * nb + sources % nb
        chosen = jnp.where(mine[:, None], matrix[local], 0.0)
        sent = lax.dynamic_slice_in_dim(chosen, (1 - core) * nb, nb, 0)
        kept = lax.dynamic_slice_in_dim(chosen, core * nb, nb, 0)
        half = kept + lax.ppermute(sent, "prow", other_core())
        piece, half = lax.optimization_barrier((piece, half))
        total = lax.dynamic_slice_in_dim(half, y * share, share, 0)
        olds = [matrix[:share]]
        for step in range(1, NY):
            to = (y + step) % NY * share
            packed = jnp.concatenate(
                [
                    lax.dynamic_slice_in_dim(half, to, share, 0),
                    lax.dynamic_slice_in_dim(matrix, to, share, 0),
                ]
            )
            got = lax.ppermute(packed, "prow", along_y(step))
            total = total + got[:share]
            olds.append(got[share:])
        slab = jnp.concatenate([total, pick(y, olds)])
    with jax.named_scope("panel_across"):
        piece = across_x(x, piece)
    piece, slab = lax.optimization_barrier((piece, slab))

    def ring(up, down):
        with jax.named_scope("panel_ring"):
            return (
                lax.ppermute(up, "pcol", along_z(1)),
                lax.ppermute(down, "pcol", along_z(-1)),
            )

    up1, down1 = ring(piece, piece)
    with jax.named_scope("fix_down"):
        fix = down_z(z, [slab[:, :nb]] * NZ)
    up1, down1, fix, origin = lax.optimization_barrier((up1, down1, fix, origin))
    up2, down2 = ring(up1, down1)
    with jax.named_scope("fix_across"):
        fix = across_x(x, fix)
    with jax.named_scope("top_gather"):
        top_mine = gather_y(slab)
    up2, down2, fix, top_mine = lax.optimization_barrier((up2, down2, fix, top_mine))
    up3, down3 = ring(up2, down2)
    with jax.named_scope("fix_gather"):
        fix_mine = gather_y(fix)
    up3, down3, fix_mine = lax.optimization_barrier((up3, down3, fix_mine))
    up4, down4 = ring(up3[: nb // 2], down3[nb // 2 :])
    with jax.named_scope("core_gather"):
        top_other = lax.ppermute(top_mine, "prow", other_core())
        fix_other = lax.ppermute(fix_mine, "prow", other_core())

    width = matrix.shape[1]
    ids = jnp.stack([p, q, y, core]).astype(jnp.int32)
    vmem = pl.BlockSpec(memory_space=pltpu.VMEM)
    smem = pl.BlockSpec(memory_space=pltpu.SMEM)
    hbm = pl.BlockSpec(memory_space=pltpu.HBM)
    small = jax.ShapeDtypeStruct((2 * nb, width), jnp.bfloat16)
    with jax.named_scope("factor"):
        parts = pl.pallas_call(
            factor_kernel,
            out_shape=[small] * 4 + [jax.ShapeDtypeStruct((nb, width), jnp.float32)],
            in_specs=[smem] + [vmem] * 6,
            out_specs=[vmem] * 5,
            compiler_params=pltpu.CompilerParams(vmem_limit_bytes=24 * 1024 * 1024),
            cost_estimate=pl.CostEstimate(
                flops=3 * 10**9, bytes_accessed=8 * 2**20, transcendentals=0
            ),
        )(ids, top_mine, top_other, fix_mine, fix_other, lower_inverse, upper_inverse)
    blocks = pltpu.VMEM((2, nb, width), jnp.float32)
    with jax.named_scope("update"):
        return pl.pallas_call(
            update_kernel,
            out_shape=jax.ShapeDtypeStruct((rows, width), jnp.float32),
            in_specs=[smem] + [vmem] * (6 + NZ + 1) + [hbm],
            out_specs=hbm,
            scratch_shapes=[blocks] * 2 + [pltpu.SemaphoreType.DMA((2,))] * 2,
            compiler_params=pltpu.CompilerParams(vmem_limit_bytes=24 * 1024 * 1024),
            cost_estimate=pl.CostEstimate(
                flops=6 * 10**9, bytes_accessed=14 * 2**20, transcendentals=0
            ),
        )(
            ids, origin, *parts, piece, up1, down1, up2, down2, up3, down3, up4, down4,
            pltpu.with_memory_space_constraint(matrix, pltpu.HBM),
        )


def solution(mesh):
    in_specs = (P("prow", "pcol"), P(), P(), P())
    out_specs = P("prow", "pcol")
    return jax.shard_map(
        on_device, mesh=mesh, in_specs=in_specs, out_specs=out_specs, check_vma=False
    )
```

```python
import jax
import jax.numpy as jnp
from jax import lax
from jax.experimental import pallas as pl
from jax.experimental.pallas import tpu as pltpu
from jax.sharding import PartitionSpec as P

NZ, NX, NY, NCORE = 8, 4, 4, 2


def one(left, right):
    return jnp.dot(left, right, preferred_element_type=jnp.float32)


def split(value):
    high = value.astype(jnp.bfloat16)
    return high, (value - high.astype(jnp.float32)).astype(jnp.bfloat16)


def dot(left, right):
    (left_high, left_low), (right_high, right_low) = split(left), split(right)
    return one(left_high, right_high) + one(left_high, right_low) + one(left_low, right_high)


def at(z, x):
    return z % NZ * NX + x % NX


def along_z(step):
    return [(at(z, x), at(z + step, x)) for z in range(NZ) for x in range(NX)]


def along_y(step):
    return [
        (y * NCORE + c, (y + step) % NY * NCORE + c) for y in range(NY) for c in range(NCORE)
    ]


def other_core():
    return [(y * NCORE + c, y * NCORE + 1 - c) for y in range(NY) for c in range(NCORE)]


def pick(index, options):
    value = options[0]
    for place in reversed(range(1, len(options))):
        value = jnp.where(index == place, options[place], value)
    return value


def scatter_z(z, pieces):
    arrived = [pieces[0]]
    for k in range(1, NZ):
        pairs = [(at(0, x), at(k, x)) for x in (0, 1)]
        arrived.append(lax.ppermute(pieces[k], "pcol", pairs))
    return arrived


def send_z(value, pairs):
    return lax.ppermute(value, "pcol", [(at(a, x), at(b, x)) for a, b in pairs for x in (0, 1)])


def spread_z(z, mine):
    mine = jnp.where(z == 4, send_z(mine, [(0, 4)]), mine)
    above = send_z(mine, [(0, 1), (4, 3)])
    below = send_z(mine, [(0, 7), (4, 5)])
    between = send_z(mine, [(0, 2), (4, 6)])
    return pick(z, [mine, above, between, above, mine, below, between, below])


def across_x(x, mine):
    def both(to_first, to_second):
        return [(at(z, 0), at(z, to_first)) for z in range(NZ)] + [
            (at(z, 1), at(z, to_second)) for z in range(NZ)
        ]

    plus = lax.ppermute(mine, "pcol", both(1, 2))
    minus = lax.ppermute(mine, "pcol", both(3, 0))
    twice = lax.ppermute(mine, "pcol", both(2, 3))
    first = pick(x, [mine, plus, twice, minus])
    second = pick(x, [minus, mine, plus, twice])
    return jnp.concatenate([first, second], axis=1)


def gather_y(mine):
    return jnp.stack([mine] + [lax.ppermute(mine, "prow", along_y(k)) for k in range(1, NY)])


def factor_kernel(
    ids, top_mine, top_other, fix_mine, fix_other, lower_inverse, upper_inverse,
    factor_high, factor_low, moved_high, moved_low, head,
):
    p, q, y, core = ids[0], ids[1], ids[2], ids[3]
    nb = lower_inverse.shape[1]
    share = top_mine.shape[1] // 2
    width = top_mine.shape[2]

    def rows(mine, other, which, part):
        held = []
        for owner in range(NY):
            back = lax.rem(y - owner + NY, NY)
            held.append(
                jnp.where(
                    core == which,
                    mine[back, part * share : (part + 1) * share, :],
                    other[back, part * share : (part + 1) * share, :],
                )
            )
        return jnp.concatenate(held, axis=0)

    first, second = rows(top_mine, top_other, 0, 0), rows(top_mine, top_other, 1, 0)
    cross_rows = rows(fix_mine, fix_other, 0, 0)[:, nb:]
    panel_rows = rows(fix_mine, fix_other, 1, 0)[:, :nb]
    row = lax.broadcasted_iota(jnp.int32, (nb, width), 0)
    column = lax.broadcasted_iota(jnp.int32, (nb, width), 1)
    in_first = jnp.logical_and(q == 0, column < nb)
    in_second = jnp.logical_and(q == 1, column < nb)
    minus_one = jnp.where(row == column, -1.0, 0.0).astype(jnp.float32)
    upper0 = dot(lower_inverse[0], first)
    lower_top = dot(panel_rows, upper_inverse[0])
    cross = dot(lower_inverse[0], cross_rows)
    swapped1 = second - dot(lower_top, upper0)
    upper1 = dot(lower_inverse[1], swapped1)
    use0 = jnp.where(in_first, minus_one, jnp.where(in_second, 0.0, upper0))
    use1 = jnp.where(in_second, minus_one, jnp.where(in_first, 0.0, upper1))
    solved1 = dot(upper_inverse[1], use1)
    solved0 = dot(upper_inverse[0], use0 - dot(cross, solved1))
    high0, low0 = split(solved0)
    high1, low1 = split(solved1)
    factor_high[:nb], factor_high[nb:] = high0, high1
    factor_low[:nb], factor_low[nb:] = low0, low1
    lower_wide = jnp.concatenate([lower_top] * (width // nb), axis=1)
    top0 = jnp.where(in_first, first, upper0)
    top1 = jnp.where(in_first, lower_wide, jnp.where(in_second, swapped1, upper1))
    head[...] = jnp.where(p == 0, top0, top1)
    drop = jnp.logical_or(in_first, in_second)
    for which in range(NCORE):
        old = jnp.where(drop, 0.0, rows(top_mine, top_other, which, 1))
        panel_part = rows(fix_mine, fix_other, which, 1)
        moved = old - dot(panel_part[:, :nb], solved0) - dot(panel_part[:, nb:], solved1)
        high, low = split(moved)
        moved_high[which * nb : (which + 1) * nb] = high
        moved_low[which * nb : (which + 1) * nb] = low


def update_kernel(
    ids, origin, factor_high, factor_low, moved_high, moved_low, head, *rest
):
    pieces = rest[: NZ + 1]
    matrix, out, matrix_block, out_block, matrix_sem, out_sem = rest[NZ + 1 :]
    p, q = ids[0], ids[1]
    z = lax.div(q, NX)
    nb, width = head.shape
    column = lax.broadcasted_iota(jnp.int32, (nb, width), 1)
    drop = jnp.logical_and(q < 2, column < nb)
    owners = [lax.rem(z + step + NZ, NZ) for step in (0, -1, 1, -2, 2, -3, 3, NZ // 2)]

    def place(i):
        return pl.ds(pl.multiple_of(owners[i] * nb, nb), nb)

    def part(i):
        return pl.ds(i % 4 * nb, nb)

    def matrix_copy(i):
        return pltpu.make_async_copy(
            matrix.at[place(i)], matrix_block.at[part(i)], matrix_sem.at[i % 4]
        )

    def out_copy(i):
        return pltpu.make_async_copy(out_block.at[part(i)], out.at[place(i)], out_sem.at[i % 4])

    for i in range(4):
        matrix_copy(i).start()
    for i in range(0, NZ, 2):
        held = [pieces[i][...], pieces[i + 1][...]]
        if i + 2 == NZ:
            held.append(pieces[i + 2][...])
        high, low = split(jnp.concatenate(held, axis=0))
        product = (
            one(high, factor_high[...]) + one(high, factor_low[...]) + one(low, factor_high[...])
        )
        source = jnp.concatenate([origin[place(i), :], origin[place(i + 1), :]], axis=0)
        places = lax.broadcasted_iota(jnp.int32, (2 * nb, 2 * nb), 1)
        chosen = jnp.where(source == places, 1.0, 0.0).astype(jnp.bfloat16)
        moved = one(chosen, moved_high[...]) + one(chosen, moved_low[...])
        for j in (i, i + 1):
            here = slice((j - i) * nb, (j - i + 1) * nb)
            matrix_copy(j).wait()
            if j >= 4:
                out_copy(j - 4).wait()
            kept = jnp.where(drop, 0.0, matrix_block[part(j)]) - product[here]
            value = jnp.where(source[here] >= 0, moved[here], kept)
            is_head = jnp.logical_and(owners[j] == 0, p < 2)
            out_block[part(j)] = jnp.where(is_head, head[...], value)
            out_copy(j).start()
            if j + 4 < NZ:
                matrix_copy(j + 4).start()
    for i in range(NZ - 4, NZ):
        out_copy(i).wait()


def on_device(matrix, pivots, lower_inverse, upper_inverse):
    nb = lower_inverse.shape[1]
    rows = matrix.shape[0]
    n_prow = lax.axis_size("prow")
    p, q = lax.axis_index("prow"), lax.axis_index("pcol")
    y, core = p // NCORE, p % NCORE
    z, x = q // NX, q % NX
    share = 2 * nb // n_prow

    with jax.named_scope("panel_scatter"):
        arrived = scatter_z(z, [matrix[nb * k : nb * (k + 1), :nb] for k in range(NZ)])

    order = jnp.arange(nb, dtype=jnp.int32)

    def before0(pivot0, wanted):
        hit = wanted[:, None] == pivot0[None, :]
        found = jnp.sum(jnp.where(hit, order[None, :] + 1, 0), axis=1)
        return jnp.where(found > 0, found - 1, wanted)

    def origin_of(pivots):
        second_top = before0(pivots[0], nb + order)
        place = lax.broadcasted_iota(jnp.int32, (rows, 1), 0)
        row_ids = (place // nb * n_prow + p) * nb + place % nb
        hit1 = row_ids == pivots[1][None, :]
        hit0 = row_ids == pivots[0][None, :]
        from1 = jnp.sum(jnp.where(hit1, second_top[None, :] + 1, 0), axis=1, keepdims=True)
        from0 = jnp.sum(jnp.where(hit0, order[None, :] + 1, 0), axis=1, keepdims=True)
        return jnp.where(row_ids >= 2 * nb, jnp.where(from1 > 0, from1, from0), 0) - 1

    sources = jnp.concatenate([pivots[0], before0(pivots[0], pivots[1])])

    with jax.named_scope("top_exchange"):
        mine = sources // nb % n_prow == p
        local = sources // nb // n_prow * nb + sources % nb
        chosen = jnp.where(mine[:, None], matrix[local], 0.0)
        sent = lax.dynamic_slice_in_dim(chosen, (1 - core) * nb, nb, 0)
        kept = lax.dynamic_slice_in_dim(chosen, core * nb, nb, 0)
        half = kept + lax.ppermute(sent, "prow", other_core())
        piece, half = lax.optimization_barrier((pick(z, arrived), half))
        total = lax.dynamic_slice_in_dim(half, y * share, share, 0)
        olds = [matrix[:share]]
        for step in range(1, NY):
            to = (y + step) % NY * share
            packed = jnp.concatenate(
                [
                    lax.dynamic_slice_in_dim(half, to, share, 0),
                    lax.dynamic_slice_in_dim(matrix, to, share, 0),
                ]
            )
            got = lax.ppermute(packed, "prow", along_y(step))
            total = total + got[:share]
            olds.append(got[share:])
        slab = jnp.concatenate([total, pick(y, olds)])

    def ring(up, down):
        with jax.named_scope("panel_ring"):
            return (
                lax.ppermute(up, "pcol", along_z(1)),
                lax.ppermute(down, "pcol", along_z(-1)),
            )

    with jax.named_scope("panel_across"):
        piece = across_x(x, piece)
    piece, slab, pivots = lax.optimization_barrier((piece, slab, pivots))
    up1, down1 = ring(piece, piece)
    with jax.named_scope("fix_down"):
        fix = spread_z(z, slab[:, :nb])
    origin = origin_of(pivots)
    fix, origin, _ = lax.optimization_barrier((fix, origin, up1))
    up2, down2 = ring(up1, down1)
    with jax.named_scope("fix_across"):
        fix = across_x(x, fix)
    with jax.named_scope("top_gather"):
        top_mine = gather_y(slab)
    fix, top_mine, _ = lax.optimization_barrier((fix, top_mine, up2))
    up3, down3 = ring(up2, down2)
    with jax.named_scope("fix_gather"):
        fix_mine = gather_y(fix)
    up3, down3, fix_mine = lax.optimization_barrier((up3, down3, fix_mine))
    up4, down4 = ring(up3[: nb // 2], down3[nb // 2 :])
    with jax.named_scope("core_gather"):
        top_other = lax.ppermute(top_mine, "prow", other_core())
        fix_other = lax.ppermute(fix_mine, "prow", other_core())

    width = matrix.shape[1]
    ids = jnp.stack([p, q, y, core]).astype(jnp.int32)
    vmem = pl.BlockSpec(memory_space=pltpu.VMEM)
    smem = pl.BlockSpec(memory_space=pltpu.SMEM)
    hbm = pl.BlockSpec(memory_space=pltpu.HBM)
    small = jax.ShapeDtypeStruct((2 * nb, width), jnp.bfloat16)
    with jax.named_scope("factor"):
        parts = pl.pallas_call(
            factor_kernel,
            out_shape=[small] * 4 + [jax.ShapeDtypeStruct((nb, width), jnp.float32)],
            in_specs=[smem] + [vmem] * 6,
            out_specs=[vmem] * 5,
            compiler_params=pltpu.CompilerParams(vmem_limit_bytes=24 * 1024 * 1024),
            cost_estimate=pl.CostEstimate(
                flops=3 * 10**9, bytes_accessed=8 * 2**20, transcendentals=0
            ),
        )(ids, top_mine, top_other, fix_mine, fix_other, lower_inverse, upper_inverse)
    blocks = pltpu.VMEM((4 * nb, width), jnp.float32)
    with jax.named_scope("update"):
        return pl.pallas_call(
            update_kernel,
            out_shape=jax.ShapeDtypeStruct((rows, width), jnp.float32),
            in_specs=[smem] + [vmem] * (6 + NZ + 1) + [hbm],
            out_specs=hbm,
            scratch_shapes=[blocks] * 2 + [pltpu.SemaphoreType.DMA((4,))] * 2,
            compiler_params=pltpu.CompilerParams(vmem_limit_bytes=24 * 1024 * 1024),
            cost_estimate=pl.CostEstimate(
                flops=6 * 10**9, bytes_accessed=14 * 2**20, transcendentals=0
            ),
        )(
            ids, origin, *parts, piece, up1, down1, up2, down2, up3, down3, up4, down4,
            pltpu.with_memory_space_constraint(matrix, pltpu.HBM),
        )


def solution(mesh):
    in_specs = (P("prow", "pcol"), P(), P(), P())
    out_specs = P("prow", "pcol")
    return jax.shard_map(
        on_device, mesh=mesh, in_specs=in_specs, out_specs=out_specs, check_vma=False
    )
```

```python
import jax
import jax.numpy as jnp
from jax import lax
from jax.experimental import pallas as pl
from jax.experimental.pallas import tpu as pltpu
from jax.sharding import PartitionSpec as P

NZ, NX, NY, NCORE = 8, 4, 4, 2


def one(left, right):
    return jnp.dot(left, right, preferred_element_type=jnp.float32)


def split(value):
    high = value.astype(jnp.bfloat16)
    return high, (value - high.astype(jnp.float32)).astype(jnp.bfloat16)


def dot(left, right):
    (left_high, left_low), (right_high, right_low) = split(left), split(right)
    return one(left_high, right_high) + one(left_high, right_low) + one(left_low, right_high)


def at(z, x):
    return z % NZ * NX + x % NX


def along_z(step):
    return [(at(z, x), at(z + step, x)) for z in range(NZ) for x in range(NX)]


def along_y(step):
    return [
        (y * NCORE + c, (y + step) % NY * NCORE + c) for y in range(NY) for c in range(NCORE)
    ]


def other_core():
    return [(y * NCORE + c, y * NCORE + 1 - c) for y in range(NY) for c in range(NCORE)]


def pick(index, options):
    value = options[0]
    for place in reversed(range(1, len(options))):
        value = jnp.where(index == place, options[place], value)
    return value


def scatter_z(z, pieces):
    arrived = [pieces[0]]
    for k in range(1, NZ):
        pairs = [(at(0, x), at(k, x)) for x in (0, 1)]
        arrived.append(lax.ppermute(pieces[k], "pcol", pairs))
    return arrived


def send_z(value, pairs):
    return lax.ppermute(value, "pcol", [(at(a, x), at(b, x)) for a, b in pairs for x in (0, 1)])


def half_way_z(z, mine):
    return jnp.where(z == 4, send_z(mine, [(0, 4)]), mine)


def rest_of_z(z, mine):
    above = send_z(mine, [(0, 1), (4, 3)])
    below = send_z(mine, [(0, 7), (4, 5)])
    between = send_z(mine, [(0, 2), (4, 6)])
    return pick(z, [mine, above, between, above, mine, below, between, below])


def across_x(x, mine):
    def both(to_first, to_second):
        return [(at(z, 0), at(z, to_first)) for z in range(NZ)] + [
            (at(z, 1), at(z, to_second)) for z in range(NZ)
        ]

    plus = lax.ppermute(mine, "pcol", both(1, 2))
    minus = lax.ppermute(mine, "pcol", both(3, 0))
    twice = lax.ppermute(mine, "pcol", both(2, 3))
    first = pick(x, [mine, plus, twice, minus])
    second = pick(x, [minus, mine, plus, twice])
    return jnp.concatenate([first, second], axis=1)


def gather_y(mine):
    return jnp.stack([mine] + [lax.ppermute(mine, "prow", along_y(k)) for k in range(1, NY)])


def factor_kernel(
    ids, top_mine, top_other, fix_mine, fix_other, lower_inverse, upper_inverse,
    factor_high, factor_low, moved_high, moved_low, head,
):
    p, q, y, core = ids[0], ids[1], ids[2], ids[3]
    nb = lower_inverse.shape[1]
    share = top_mine.shape[1] // 2
    width = top_mine.shape[2]

    def rows(mine, other, which, part):
        held = []
        for owner in range(NY):
            back = lax.rem(y - owner + NY, NY)
            held.append(
                jnp.where(
                    core == which,
                    mine[back, part * share : (part + 1) * share, :],
                    other[back, part * share : (part + 1) * share, :],
                )
            )
        return jnp.concatenate(held, axis=0)

    first, second = rows(top_mine, top_other, 0, 0), rows(top_mine, top_other, 1, 0)
    cross_rows = rows(fix_mine, fix_other, 0, 0)[:, nb:]
    panel_rows = rows(fix_mine, fix_other, 1, 0)[:, :nb]
    row = lax.broadcasted_iota(jnp.int32, (nb, width), 0)
    column = lax.broadcasted_iota(jnp.int32, (nb, width), 1)
    in_first = jnp.logical_and(q == 0, column < nb)
    in_second = jnp.logical_and(q == 1, column < nb)
    minus_one = jnp.where(row == column, -1.0, 0.0).astype(jnp.float32)
    upper0 = dot(lower_inverse[0], first)
    lower_top = dot(panel_rows, upper_inverse[0])
    cross = dot(lower_inverse[0], cross_rows)
    swapped1 = second - dot(lower_top, upper0)
    upper1 = dot(lower_inverse[1], swapped1)
    use0 = jnp.where(in_first, minus_one, jnp.where(in_second, 0.0, upper0))
    use1 = jnp.where(in_second, minus_one, jnp.where(in_first, 0.0, upper1))
    solved1 = dot(upper_inverse[1], use1)
    solved0 = dot(upper_inverse[0], use0 - dot(cross, solved1))
    high0, low0 = split(solved0)
    high1, low1 = split(solved1)
    factor_high[:nb], factor_high[nb:] = high0, high1
    factor_low[:nb], factor_low[nb:] = low0, low1
    lower_wide = jnp.concatenate([lower_top] * (width // nb), axis=1)
    top0 = jnp.where(in_first, first, upper0)
    top1 = jnp.where(in_first, lower_wide, jnp.where(in_second, swapped1, upper1))
    head[...] = jnp.where(p == 0, top0, top1)
    drop = jnp.logical_or(in_first, in_second)
    for which in range(NCORE):
        old = jnp.where(drop, 0.0, rows(top_mine, top_other, which, 1))
        panel_part = rows(fix_mine, fix_other, which, 1)
        moved = old - dot(panel_part[:, :nb], solved0) - dot(panel_part[:, nb:], solved1)
        high, low = split(moved)
        moved_high[which * nb : (which + 1) * nb] = high
        moved_low[which * nb : (which + 1) * nb] = low


def update_kernel(
    ids, origin, factor_high, factor_low, moved_high, moved_low, head, *rest
):
    pieces = rest[: NZ + 1]
    matrix, out, out_block, out_sem = rest[NZ + 1 :]
    p, q = ids[0], ids[1]
    z = lax.div(q, NX)
    nb, width = head.shape
    column = lax.broadcasted_iota(jnp.int32, (nb, width), 1)
    drop = jnp.logical_and(q < 2, column < nb)
    owners = [lax.rem(z + step + NZ, NZ) for step in (0, -1, 1, -2, 2, -3, 3, NZ // 2)]

    def place(i):
        return pl.ds(pl.multiple_of(owners[i] * nb, nb), nb)

    def part(i):
        return pl.ds(i % 4 * nb, nb)

    def out_copy(i):
        return pltpu.make_async_copy(out_block.at[part(i)], out.at[place(i)], out_sem.at[i % 4])

    for i in range(0, NZ, 2):
        held = [pieces[i][...], pieces[i + 1][...]]
        if i + 2 == NZ:
            held.append(pieces[i + 2][...])
        high, low = split(jnp.concatenate(held, axis=0))
        product = (
            one(high, factor_high[...]) + one(high, factor_low[...]) + one(low, factor_high[...])
        )
        source = jnp.concatenate([origin[place(i), :], origin[place(i + 1), :]], axis=0)
        places = lax.broadcasted_iota(jnp.int32, (2 * nb, 2 * nb), 1)
        chosen = jnp.where(source == places, 1.0, 0.0).astype(jnp.bfloat16)
        moved = one(chosen, moved_high[...]) + one(chosen, moved_low[...])
        for j in (i, i + 1):
            here = slice((j - i) * nb, (j - i + 1) * nb)
            if j >= 4:
                out_copy(j - 4).wait()
            kept = jnp.where(drop, 0.0, matrix[place(j), :]) - product[here]
            value = jnp.where(source[here] >= 0, moved[here], kept)
            is_head = jnp.logical_and(owners[j] == 0, p < 2)
            out_block[part(j)] = jnp.where(is_head, head[...], value)
            out_copy(j).start()
    for i in range(NZ - 4, NZ):
        out_copy(i).wait()


def on_device(matrix, pivots, lower_inverse, upper_inverse):
    nb = lower_inverse.shape[1]
    rows = matrix.shape[0]
    n_prow = lax.axis_size("prow")
    p, q = lax.axis_index("prow"), lax.axis_index("pcol")
    y, core = p // NCORE, p % NCORE
    z, x = q // NX, q % NX
    share = 2 * nb // n_prow

    with jax.named_scope("panel_scatter"):
        arrived = scatter_z(z, [matrix[nb * k : nb * (k + 1), :nb] for k in range(NZ)])

    order = jnp.arange(nb, dtype=jnp.int32)

    def before0(pivot0, wanted):
        hit = wanted[:, None] == pivot0[None, :]
        found = jnp.sum(jnp.where(hit, order[None, :] + 1, 0), axis=1)
        return jnp.where(found > 0, found - 1, wanted)

    def origin_of(pivots):
        second_top = before0(pivots[0], nb + order)
        place = lax.broadcasted_iota(jnp.int32, (rows, 1), 0)
        row_ids = (place // nb * n_prow + p) * nb + place % nb
        hit1 = row_ids == pivots[1][None, :]
        hit0 = row_ids == pivots[0][None, :]
        from1 = jnp.sum(jnp.where(hit1, second_top[None, :] + 1, 0), axis=1, keepdims=True)
        from0 = jnp.sum(jnp.where(hit0, order[None, :] + 1, 0), axis=1, keepdims=True)
        return jnp.where(row_ids >= 2 * nb, jnp.where(from1 > 0, from1, from0), 0) - 1

    sources = jnp.concatenate([pivots[0], before0(pivots[0], pivots[1])])

    with jax.named_scope("top_exchange"):
        mine = sources // nb % n_prow == p
        local = sources // nb // n_prow * nb + sources % nb
        chosen = jnp.where(mine[:, None], matrix[local], 0.0)
        sent = lax.dynamic_slice_in_dim(chosen, (1 - core) * nb, nb, 0)
        kept = lax.dynamic_slice_in_dim(chosen, core * nb, nb, 0)
        half = kept + lax.ppermute(sent, "prow", other_core())
        piece, half = lax.optimization_barrier((pick(z, arrived), half))
        total = lax.dynamic_slice_in_dim(half, y * share, share, 0)
        olds = [matrix[:share]]
        for step in range(1, NY):
            to = (y + step) % NY * share
            packed = jnp.concatenate(
                [
                    lax.dynamic_slice_in_dim(half, to, share, 0),
                    lax.dynamic_slice_in_dim(matrix, to, share, 0),
                ]
            )
            got = lax.ppermute(packed, "prow", along_y(step))
            total = total + got[:share]
            olds.append(got[share:])
        slab = jnp.concatenate([total, pick(y, olds)])

    def ring(up, down):
        with jax.named_scope("panel_ring"):
            return (
                lax.ppermute(up, "pcol", along_z(1)),
                lax.ppermute(down, "pcol", along_z(-1)),
            )

    with jax.named_scope("panel_across"):
        piece = across_x(x, piece)
    with jax.named_scope("fix_half"):
        fix = half_way_z(z, slab[:, :nb])
    piece, fix, pivots = lax.optimization_barrier((piece, fix, pivots))
    up1, down1 = ring(piece, piece)
    with jax.named_scope("fix_down"):
        fix = rest_of_z(z, fix)
    origin = origin_of(pivots)
    fix, origin, _ = lax.optimization_barrier((fix, origin, up1))
    up2, down2 = ring(up1, down1)
    with jax.named_scope("fix_across"):
        fix = across_x(x, fix)
    with jax.named_scope("top_gather"):
        top_mine = gather_y(slab)
    fix, top_mine, _ = lax.optimization_barrier((fix, top_mine, up2))
    up3, down3 = ring(up2, down2)
    with jax.named_scope("fix_gather"):
        fix_mine = gather_y(fix)
    up3, down3, fix_mine = lax.optimization_barrier((up3, down3, fix_mine))
    up4, down4 = ring(up3[: nb // 2], down3[nb // 2 :])
    with jax.named_scope("core_gather"):
        top_other = lax.ppermute(top_mine, "prow", other_core())
        fix_other = lax.ppermute(fix_mine, "prow", other_core())

    width = matrix.shape[1]
    ids = jnp.stack([p, q, y, core]).astype(jnp.int32)
    vmem = pl.BlockSpec(memory_space=pltpu.VMEM)
    smem = pl.BlockSpec(memory_space=pltpu.SMEM)
    hbm = pl.BlockSpec(memory_space=pltpu.HBM)
    small = jax.ShapeDtypeStruct((2 * nb, width), jnp.bfloat16)
    with jax.named_scope("factor"):
        parts = pl.pallas_call(
            factor_kernel,
            out_shape=[small] * 4 + [jax.ShapeDtypeStruct((nb, width), jnp.float32)],
            in_specs=[smem] + [vmem] * 6,
            out_specs=[vmem] * 5,
            compiler_params=pltpu.CompilerParams(vmem_limit_bytes=16 * 1024 * 1024),
            cost_estimate=pl.CostEstimate(
                flops=3 * 10**9, bytes_accessed=8 * 2**20, transcendentals=0
            ),
        )(ids, top_mine, top_other, fix_mine, fix_other, lower_inverse, upper_inverse)
    blocks = pltpu.VMEM((4 * nb, width), jnp.float32)
    with jax.named_scope("update"):
        return pl.pallas_call(
            update_kernel,
            out_shape=jax.ShapeDtypeStruct((rows, width), jnp.float32),
            in_specs=[smem] + [vmem] * (6 + NZ + 2),
            out_specs=hbm,
            scratch_shapes=[blocks, pltpu.SemaphoreType.DMA((4,))],
            compiler_params=pltpu.CompilerParams(vmem_limit_bytes=16 * 1024 * 1024),
            cost_estimate=pl.CostEstimate(
                flops=6 * 10**9, bytes_accessed=14 * 2**20, transcendentals=0
            ),
        )(
            ids, origin, *parts, piece, up1, down1, up2, down2, up3, down3, up4, down4,
            matrix,
        )


def solution(mesh):
    in_specs = (P("prow", "pcol"), P(), P(), P())
    out_specs = P("prow", "pcol")
    return jax.shard_map(
        on_device, mesh=mesh, in_specs=in_specs, out_specs=out_specs, check_vma=False
    )
```

```python
import jax
import jax.numpy as jnp
from jax import lax
from jax.experimental import pallas as pl
from jax.experimental.pallas import tpu as pltpu
from jax.sharding import PartitionSpec as P

NZ, NX, NY, NCORE = 8, 4, 4, 2


def one(left, right):
    return jnp.dot(left, right, preferred_element_type=jnp.float32)


def split(value):
    high = value.astype(jnp.bfloat16)
    return high, (value - high.astype(jnp.float32)).astype(jnp.bfloat16)


def dot(left, right):
    (left_high, left_low), (right_high, right_low) = split(left), split(right)
    return one(left_high, right_high) + one(left_high, right_low) + one(left_low, right_high)


def at(z, x):
    return z % NZ * NX + x % NX


def along_z(step):
    return [(at(z, x), at(z + step, x)) for z in range(NZ) for x in range(NX)]


def along_y(step):
    return [
        (y * NCORE + c, (y + step) % NY * NCORE + c) for y in range(NY) for c in range(NCORE)
    ]


def other_core():
    return [(y * NCORE + c, y * NCORE + 1 - c) for y in range(NY) for c in range(NCORE)]


def pick(index, options):
    value = options[0]
    for place in reversed(range(1, len(options))):
        value = jnp.where(index == place, options[place], value)
    return value


def scatter_z(z, pieces):
    arrived = [pieces[0]]
    for k in range(1, NZ):
        pairs = [(at(0, x), at(k, x)) for x in (0, 1)]
        arrived.append(lax.ppermute(pieces[k], "pcol", pairs))
    return arrived


def send_z(value, pairs):
    return lax.ppermute(value, "pcol", [(at(a, x), at(b, x)) for a, b in pairs for x in (0, 1)])


def half_way_z(z, mine):
    return jnp.where(z == 4, send_z(mine, [(0, 4)]), mine)


def rest_of_z(z, mine):
    above = send_z(mine, [(0, 1), (4, 3)])
    below = send_z(mine, [(0, 7), (4, 5)])
    between = send_z(mine, [(0, 2), (4, 6)])
    return pick(z, [mine, above, between, above, mine, below, between, below])


def across_x(x, mine):
    def both(to_first, to_second):
        return [(at(z, 0), at(z, to_first)) for z in range(NZ)] + [
            (at(z, 1), at(z, to_second)) for z in range(NZ)
        ]

    plus = lax.ppermute(mine, "pcol", both(1, 2))
    minus = lax.ppermute(mine, "pcol", both(3, 0))
    twice = lax.ppermute(mine, "pcol", both(2, 3))
    first = pick(x, [mine, plus, twice, minus])
    second = pick(x, [minus, mine, plus, twice])
    return jnp.concatenate([first, second], axis=1)


def gather_y(mine):
    return jnp.stack([mine] + [lax.ppermute(mine, "prow", along_y(k)) for k in range(1, NY)])


def factor_kernel(
    ids, top_mine, top_other, fix_mine, fix_other, lower_inverse, upper_inverse,
    factor_high, factor_low, moved_high, moved_low, head,
):
    p, q, y, core = ids[0], ids[1], ids[2], ids[3]
    nb = lower_inverse.shape[1]
    share = top_mine.shape[1] // 2
    width = top_mine.shape[2]

    def rows(mine, other, which, part):
        held = []
        for owner in range(NY):
            back = lax.rem(y - owner + NY, NY)
            held.append(
                jnp.where(
                    core == which,
                    mine[back, part * share : (part + 1) * share, :],
                    other[back, part * share : (part + 1) * share, :],
                )
            )
        return jnp.concatenate(held, axis=0)

    first, second = rows(top_mine, top_other, 0, 0), rows(top_mine, top_other, 1, 0)
    cross_rows = rows(fix_mine, fix_other, 0, 0)[:, nb:]
    panel_rows = rows(fix_mine, fix_other, 1, 0)[:, :nb]
    row = lax.broadcasted_iota(jnp.int32, (nb, width), 0)
    column = lax.broadcasted_iota(jnp.int32, (nb, width), 1)
    in_first = jnp.logical_and(q == 0, column < nb)
    in_second = jnp.logical_and(q == 1, column < nb)
    minus_one = jnp.where(row == column, -1.0, 0.0).astype(jnp.float32)
    upper0 = dot(lower_inverse[0], first)
    lower_top = dot(panel_rows, upper_inverse[0])
    cross = dot(lower_inverse[0], cross_rows)
    swapped1 = second - dot(lower_top, upper0)
    upper1 = dot(lower_inverse[1], swapped1)
    use0 = jnp.where(in_first, minus_one, jnp.where(in_second, 0.0, upper0))
    use1 = jnp.where(in_second, minus_one, jnp.where(in_first, 0.0, upper1))
    solved1 = dot(upper_inverse[1], use1)
    solved0 = dot(upper_inverse[0], use0 - dot(cross, solved1))
    high0, low0 = split(solved0)
    high1, low1 = split(solved1)
    factor_high[:nb], factor_high[nb:] = high0, high1
    factor_low[:nb], factor_low[nb:] = low0, low1
    lower_wide = jnp.concatenate([lower_top] * (width // nb), axis=1)
    top0 = jnp.where(in_first, first, upper0)
    top1 = jnp.where(in_first, lower_wide, jnp.where(in_second, swapped1, upper1))
    head[...] = jnp.where(p == 0, top0, top1)
    drop = jnp.logical_or(in_first, in_second)
    for which in range(NCORE):
        old = jnp.where(drop, 0.0, rows(top_mine, top_other, which, 1))
        panel_part = rows(fix_mine, fix_other, which, 1)
        moved = old - dot(panel_part[:, :nb], solved0) - dot(panel_part[:, nb:], solved1)
        high, low = split(moved)
        moved_high[which * nb : (which + 1) * nb] = high
        moved_low[which * nb : (which + 1) * nb] = low


def update_kernel(
    ids, origin, factor_high, factor_low, moved_high, moved_low, head, *rest
):
    pieces = rest[: NZ + 1]
    matrix, out, out_block, out_sem = rest[NZ + 1 :]
    p, q = ids[0], ids[1]
    z = lax.div(q, NX)
    nb, width = head.shape
    column = lax.broadcasted_iota(jnp.int32, (nb, width), 1)
    drop = jnp.logical_and(q < 2, column < nb)
    owners = [lax.rem(z + step + NZ, NZ) for step in (0, -1, 1, -2, 2, -3, 3, NZ // 2)]

    def place(i):
        return pl.ds(pl.multiple_of(owners[i] * nb, nb), nb)

    def part(i):
        return pl.ds(i * nb, nb)

    def out_copy(i):
        return pltpu.make_async_copy(out_block.at[part(i)], out.at[place(i)], out_sem.at[i])

    for i in range(0, NZ, 2):
        held = [pieces[i][...], pieces[i + 1][...]]
        if i + 2 == NZ:
            held.append(pieces[i + 2][...])
        high, low = split(jnp.concatenate(held, axis=0))
        product = (
            one(high, factor_high[...]) + one(high, factor_low[...]) + one(low, factor_high[...])
        )
        source = jnp.concatenate([origin[place(i), :], origin[place(i + 1), :]], axis=0)
        places = lax.broadcasted_iota(jnp.int32, (2 * nb, 2 * nb), 1)
        chosen = jnp.where(source == places, 1.0, 0.0).astype(jnp.bfloat16)
        moved = one(chosen, moved_high[...]) + one(chosen, moved_low[...])
        for j in (i, i + 1):
            here = slice((j - i) * nb, (j - i + 1) * nb)
            kept = jnp.where(drop, 0.0, matrix[place(j), :]) - product[here]
            value = jnp.where(source[here] >= 0, moved[here], kept)
            is_head = jnp.logical_and(owners[j] == 0, p < 2)
            out_block[part(j)] = jnp.where(is_head, head[...], value)
            out_copy(j).start()
    for i in range(NZ):
        out_copy(i).wait()


def on_device(matrix, pivots, lower_inverse, upper_inverse):
    nb = lower_inverse.shape[1]
    rows = matrix.shape[0]
    n_prow = lax.axis_size("prow")
    p, q = lax.axis_index("prow"), lax.axis_index("pcol")
    y, core = p // NCORE, p % NCORE
    z, x = q // NX, q % NX
    share = 2 * nb // n_prow

    with jax.named_scope("panel_scatter"):
        arrived = scatter_z(z, [matrix[nb * k : nb * (k + 1), :nb] for k in range(NZ)])

    order = jnp.arange(nb, dtype=jnp.int32)

    def before0(pivot0, wanted):
        hit = wanted[:, None] == pivot0[None, :]
        found = jnp.sum(jnp.where(hit, order[None, :] + 1, 0), axis=1)
        return jnp.where(found > 0, found - 1, wanted)

    def origin_of(pivots):
        second_top = before0(pivots[0], nb + order)
        place = lax.broadcasted_iota(jnp.int32, (rows, 1), 0)
        row_ids = (place // nb * n_prow + p) * nb + place % nb
        hit1 = row_ids == pivots[1][None, :]
        hit0 = row_ids == pivots[0][None, :]
        from1 = jnp.sum(jnp.where(hit1, second_top[None, :] + 1, 0), axis=1, keepdims=True)
        from0 = jnp.sum(jnp.where(hit0, order[None, :] + 1, 0), axis=1, keepdims=True)
        return jnp.where(row_ids >= 2 * nb, jnp.where(from1 > 0, from1, from0), 0) - 1

    sources = jnp.concatenate([pivots[0], before0(pivots[0], pivots[1])])

    with jax.named_scope("top_exchange"):
        mine = sources // nb % n_prow == p
        local = sources // nb // n_prow * nb + sources % nb
        chosen = jnp.where(mine[:, None], matrix[local], 0.0)
        sent = lax.dynamic_slice_in_dim(chosen, (1 - core) * nb, nb, 0)
        kept = lax.dynamic_slice_in_dim(chosen, core * nb, nb, 0)
        half = kept + lax.ppermute(sent, "prow", other_core())
        piece, half = lax.optimization_barrier((pick(z, arrived), half))
        total = lax.dynamic_slice_in_dim(half, y * share, share, 0)
        olds = [matrix[:share]]
        for step in range(1, NY):
            to = (y + step) % NY * share
            packed = jnp.concatenate(
                [
                    lax.dynamic_slice_in_dim(half, to, share, 0),
                    lax.dynamic_slice_in_dim(matrix, to, share, 0),
                ]
            )
            got = lax.ppermute(packed, "prow", along_y(step))
            total = total + got[:share]
            olds.append(got[share:])
        slab = jnp.concatenate([total, pick(y, olds)])

    def ring(up, down):
        with jax.named_scope("panel_ring"):
            return (
                lax.ppermute(up, "pcol", along_z(1)),
                lax.ppermute(down, "pcol", along_z(-1)),
            )

    with jax.named_scope("panel_across"):
        piece = across_x(x, piece)
    with jax.named_scope("fix_half"):
        fix = half_way_z(z, slab[:, :nb])
    piece, fix, pivots = lax.optimization_barrier((piece, fix, pivots))
    up1, down1 = ring(piece, piece)
    with jax.named_scope("fix_down"):
        fix = rest_of_z(z, fix)
    origin = origin_of(pivots)
    fix, origin, _ = lax.optimization_barrier((fix, origin, up1))
    up2, down2 = ring(up1, down1)
    with jax.named_scope("fix_across"):
        fix = across_x(x, fix)
    with jax.named_scope("top_gather"):
        top_mine = gather_y(slab)
    fix, top_mine, _ = lax.optimization_barrier((fix, top_mine, up2))
    up3, down3 = ring(up2, down2)
    with jax.named_scope("fix_gather"):
        fix_mine = gather_y(fix)
    up3, down3, fix_mine = lax.optimization_barrier((up3, down3, fix_mine))
    up4, down4 = ring(up3[: nb // 2], down3[nb // 2 :])
    with jax.named_scope("core_gather"):
        top_other = lax.ppermute(top_mine, "prow", other_core())
        fix_other = lax.ppermute(fix_mine, "prow", other_core())

    width = matrix.shape[1]
    ids = jnp.stack([p, q, y, core]).astype(jnp.int32)
    vmem = pl.BlockSpec(memory_space=pltpu.VMEM)
    smem = pl.BlockSpec(memory_space=pltpu.SMEM)
    hbm = pl.BlockSpec(memory_space=pltpu.HBM)
    small = jax.ShapeDtypeStruct((2 * nb, width), jnp.bfloat16)
    with jax.named_scope("factor"):
        parts = pl.pallas_call(
            factor_kernel,
            out_shape=[small] * 4 + [jax.ShapeDtypeStruct((nb, width), jnp.float32)],
            in_specs=[smem] + [vmem] * 6,
            out_specs=[vmem] * 5,
            compiler_params=pltpu.CompilerParams(vmem_limit_bytes=20 * 1024 * 1024),
            cost_estimate=pl.CostEstimate(
                flops=3 * 10**9, bytes_accessed=8 * 2**20, transcendentals=0
            ),
        )(ids, top_mine, top_other, fix_mine, fix_other, lower_inverse, upper_inverse)
    blocks = pltpu.VMEM((NZ * nb, width), jnp.float32)
    with jax.named_scope("update"):
        return pl.pallas_call(
            update_kernel,
            out_shape=jax.ShapeDtypeStruct((rows, width), jnp.float32),
            in_specs=[smem] + [vmem] * (6 + NZ + 2),
            out_specs=hbm,
            scratch_shapes=[blocks, pltpu.SemaphoreType.DMA((NZ,))],
            compiler_params=pltpu.CompilerParams(vmem_limit_bytes=20 * 1024 * 1024),
            cost_estimate=pl.CostEstimate(
                flops=6 * 10**9, bytes_accessed=14 * 2**20, transcendentals=0
            ),
        )(
            ids, origin, *parts, piece, up1, down1, up2, down2, up3, down3, up4, down4,
            matrix,
        )


def solution(mesh):
    in_specs = (P("prow", "pcol"), P(), P(), P())
    out_specs = P("prow", "pcol")
    return jax.shard_map(
        on_device, mesh=mesh, in_specs=in_specs, out_specs=out_specs, check_vma=False
    )
```
